32 devices in a mesh: section: 2 (over y), tensor: 4 (over z), dp: 4 (over x, core).
Axes of the slice: x: 2, y: 2, z: 4, core: 2. Of those that a mesh axis runs over, the one named last changes fastest.
Arguments:
- block_input: bfloat16 [8, 1024, 1024], P('dp', 'tensor'), may hold values from -6 to 6
- cotangent: bfloat16 [8, 1024, 1024], P('dp', 'tensor'), may hold values from -6 to 6
- first_gain: bfloat16 [2, 1024], P('section'), may hold values from 0.25 to 1.75
- first_shift: bfloat16 [2, 1024], P('section'), may hold values from -1.25 to 1.25
- attend_weight: bfloat16 [2, 1024, 3, 1024], P('section', None, None, 'tensor'), may hold values from -0.1875 to 0.1875
- attend_bias: bfloat16 [2, 2, 1024], P('section', None, 'tensor'), may hold values from -3 to 3
- mixing_weight: bfloat16 [2, 1024, 1024], P('section', 'tensor'), may hold values from -1.5 to 1.5
- mixing_bias: bfloat16 [2, 1024], P('section'), may hold values from -1.25 to 1.25
- second_gain: bfloat16 [2, 1024], P('section'), may hold values from 0.25 to 1.75
- second_shift: bfloat16 [2, 1024], P('section'), may hold values from -1.25 to 1.25
- expand_weight: bfloat16 [2, 1024, 4096], P('section', None, 'tensor'), may hold values from -0.1875 to 0.1875
- expand_bias: bfloat16 [2, 4096], P('section', 'tensor'), may hold values from -1.25 to 1.25
- shrink_weight: bfloat16 [2, 1024, 4096], P('section', None, 'tensor'), may hold values from -0.09375 to 0.09375
- shrink_bias: bfloat16 [2, 1024], P('section'), may hold values from -1.25 to 1.25
Outputs:
- section_output: bfloat16 [2, 8, 1024, 1024], P('section', 'dp', 'tensor')
- input_change: bfloat16 [2, 8, 1024, 1024], P('section', 'dp', 'tensor')
- first_gain_gradient: float32 [2, 1024], P('section')
- first_shift_gradient: float32 [2, 1024], P('section')
- attend_weight_gradient: float32 [2, 1024, 3, 1024], P('section', None, None, 'tensor')
- attend_bias_gradient: float32 [2, 2, 1024], P('section', None, 'tensor')
- mixing_weight_gradient: float32 [2, 1024, 1024], P('section', 'tensor')
- mixing_bias_gradient: float32 [2, 1024], P('section')
- second_gain_gradient: float32 [2, 1024], P('section')
- second_shift_gradient: float32 [2, 1024], P('section')
- expand_weight_gradient: float32 [2, 1024, 4096], P('section', None, 'tensor')
- expand_bias_gradient: float32 [2, 4096], P('section', 'tensor')
- shrink_weight_gradient: float32 [2, 1024, 4096], P('section', None, 'tensor')
- shrink_bias_gradient: float32 [2, 1024], P('section')
The draws below stay inside these ranges and needn't reach their ends.
All inputs are finite; a program needn't handle non-finite values.
Results may differ from the reference program's by a relative error of at most 0.017.
Values may be sent and summed in bfloat16 or wider, within the bound.
A program may use at most 192 MiB of HBM per device.

```python
import jax
import jax.numpy as jnp
from jax import lax

D = 1024
H = 16
HD = 64
FF = 4096
LEN = 1024
SEQS = 8
N_SECTION = 2


def level_of(stream_key, shape, cuts, least, high):
    def one(dim, shards_of):
        steps = jax.random.uniform(jax.random.fold_in(jax.random.fold_in(stream_key, 6), dim), (shards_of,), jnp.float32, least / len(cuts), high / len(cuts))
        return jnp.repeat(jnp.exp(steps), shape[dim] // shards_of).reshape((-1,) + (1,) * (len(shape) - dim - 1))

    level = one(*cuts[0])
    for cut in cuts[1:]:
        level = level * one(*cut)
    return level


def centred(rng, extent, width, reach, pieces=(), held_as=jnp.bfloat16):
    level = level_of(rng, extent, pieces, -0.22, 0.18) if pieces else 1.0
    result = jax.random.normal(rng, extent, jnp.float32) * width * level
    return jnp.minimum(jnp.maximum(result, -reach), reach).astype(held_as)


def setup_inputs(seed: int = 0) -> dict:
    key_of = jax.random.split(jax.random.key(seed), 15)
    block_input = centred(key_of[0], (SEQS, LEN, D), 1.0, 6.0, ((0, 4), (1, 4)))
    cotangent = centred(key_of[1], (SEQS, LEN, D), 1.0, 6.0, ((0, 4), (1, 4)))
    first_gain = jnp.clip(1.0 + 0.15 * jax.random.normal(key_of[2], (N_SECTION, D), jnp.float32), 0.25, 1.75).astype(jnp.bfloat16)
    first_shift = centred(key_of[3], (N_SECTION, D), 0.2, 1.25, ((0, 2),))
    attend_weight = centred(key_of[4], (N_SECTION, D, 3, H * HD), D ** -0.5, 0.1875, ((0, 2), (3, 4)))
    attend_bias = centred(key_of[5], (N_SECTION, 2, H * HD), 0.5, 3.0, ((0, 2), (2, 4)))
    mixing_weight = centred(key_of[6], (N_SECTION, H * HD, D), (max(H * HD // 64, 1)) ** -0.5, 1.5, ((0, 2), (1, 4)))
    mixing_bias = centred(key_of[7], (N_SECTION, D), 0.2, 1.25, ((0, 2),))
    second_gain = jnp.clip(1.0 + 0.15 * jax.random.normal(key_of[8], (N_SECTION, D), jnp.float32), 0.25, 1.75).astype(jnp.bfloat16)
    second_shift = centred(key_of[9], (N_SECTION, D), 0.2, 1.25, ((0, 2),))
    expand_weight = centred(key_of[10], (N_SECTION, D, FF), D ** -0.5, 0.1875, ((0, 2), (2, 4)))
    expand_bias = centred(key_of[11], (N_SECTION, FF), 0.2, 1.25, ((0, 2), (1, 4)))
    shrink_weight = centred(key_of[12], (N_SECTION, D, FF), FF ** -0.5, 0.09375, ((0, 2), (2, 4)))
    shrink_bias = centred(key_of[13], (N_SECTION, D), 0.2, 1.25, ((0, 2),))
    return {"block_input": block_input, "cotangent": cotangent, "first_gain": first_gain, "first_shift": first_shift, "attend_weight": attend_weight, "attend_bias": attend_bias, "mixing_weight": mixing_weight, "mixing_bias": mixing_bias, "second_gain": second_gain, "second_shift": second_shift, "expand_weight": expand_weight, "expand_bias": expand_bias, "shrink_weight": shrink_weight, "shrink_bias": shrink_bias}


@jax.custom_vjp
def low(v):
    return lax.optimization_barrier(v.astype(jnp.bfloat16)).astype(jnp.float32)

@jax.custom_vjp
def low_back(v):
    return v

def low_keep(v):
    return (low(v), None)

def low_pass(kept, grad):
    return (grad,)

def back_keep(v):
    return (v, None)

def back_low(kept, grad):
    return (low(grad),)
low.defvjp(low_keep, low_pass)
low_back.defvjp(back_keep, back_low)
epsilon = 1e-05
highest = lax.Precision.HIGHEST

def layer_norm(values, gain_row, shift_row):
    center = values - lax.optimization_barrier(jnp.mean(values, axis=-1, keepdims=True))
    spread = lax.optimization_barrier(jnp.mean(center * center, axis=-1, keepdims=True))
    return center * lax.rsqrt(spread + epsilon) * gain_row + shift_row

def attention(queries, key_rows, value_rows):
    length = queries.shape[0]
    scores = jnp.einsum('qhd,khd->hqk', queries, key_rows, precision=highest) * HD ** (-0.5)
    row_ids = lax.broadcasted_iota(jnp.int32, (length, length), 0)
    col_ids = lax.broadcasted_iota(jnp.int32, (length, length), 1)
    scores = jnp.where((row_ids >= col_ids)[None], scores, -jnp.inf)
    scores = low_back(scores)
    shares = low(jax.nn.softmax(scores, axis=-1))
    blended = jnp.einsum('hqk,khd->qhd', shares, value_rows, precision=highest)
    return blended.reshape(length, -1)

def layer(residual, params):
    gain_one, shift_one, attend_weight, attend_bias, mixing_weight, mixing_bias, gain_two, shift_two, expand_weight, expand_bias, shrink_weight, shrink_bias = params
    length = residual.shape[0]
    normed = low(layer_norm(residual, gain_one, shift_one))
    offsets = jnp.stack([attend_bias[0], jnp.zeros_like(attend_bias[0]), attend_bias[1]])
    projected = jnp.einsum('td,dcj->tcj', normed, attend_weight, precision=highest) + offsets
    projected = low_back(low(projected))
    head_split = projected.reshape(length, 3, H, HD)
    blended = low_back(low(attention(head_split[:, 0], head_split[:, 1], head_split[:, 2])))
    middle = residual + low_back(jnp.dot(blended, mixing_weight, precision=highest)) + mixing_bias
    second = low(layer_norm(middle, gain_two, shift_two))
    hidden_pre = low_back(jnp.dot(second, expand_weight, precision=highest) + expand_bias)
    hidden = low(jax.nn.gelu(hidden_pre, approximate=True))
    return middle + low_back(jnp.dot(hidden, shrink_weight.T, precision=highest)) + shrink_bias

def reference(block_input, cotangent, first_gain, first_shift, attend_weight, attend_bias, mixing_weight, mixing_bias, second_gain, second_shift, expand_weight, expand_bias, shrink_weight, shrink_bias):
    params = tuple((array.astype(jnp.float32) for array in (first_gain, first_shift, attend_weight, attend_bias, mixing_weight, mixing_bias, second_gain, second_shift, expand_weight, expand_bias, shrink_weight, shrink_bias)))
    inputs = block_input.astype(jnp.float32)
    bumps = jnp.zeros_like(inputs)

    def model(model_inputs, model_bumps, model_params):
        section_one = tuple((array[0] for array in model_params))
        section_two = tuple((array[1] for array in model_params))

        def one_sequence(sequence_pair):
            sequence_input, sequence_bump = sequence_pair
            passed = low_back(low(layer(sequence_input, section_one)) + sequence_bump)
            return (layer(passed, section_two), passed)
        outputs, passed_all = lax.map(jax.checkpoint(one_sequence), (model_inputs, model_bumps))
        return (outputs, passed_all)
    outputs, back_function, passed_all = jax.vjp(model, inputs, bumps, params, has_aux=True)
    input_grad, bump_grad, param_grads = back_function(cotangent.astype(jnp.float32))
    gain_one_grad, shift_one_grad, attend_weight_grad, attend_bias_grad, mixing_weight_grad, mixing_bias_grad, gain_two_grad, shift_two_grad, expand_weight_grad, expand_bias_grad, shrink_weight_grad, shrink_bias_grad = param_grads
    section_output = jnp.stack([passed_all, outputs]).astype(jnp.bfloat16)
    input_change = jnp.stack([input_grad, bump_grad]).astype(jnp.bfloat16)
    return (section_output, input_change, gain_one_grad, shift_one_grad, attend_weight_grad, attend_bias_grad, mixing_weight_grad, mixing_bias_grad, gain_two_grad, shift_two_grad, expand_weight_grad, expand_bias_grad, shrink_weight_grad, shrink_bias_grad)
```

```python
import jax
import jax.numpy as jnp
from jax import lax
from jax.experimental import pallas as pl
from jax.experimental.pallas import tpu as pltpu
from jax.sharding import PartitionSpec as P

HD = 64
PAIR = 2 * HD
BLOCK = 256


epsilon = 1e-05
contract_rows = (((0,), (0,)), ((), ()))
contract_last = (((1,), (1,)), ((), ()))


def dot(left, right, dims=(((1,), (0,)), ((), ()))):
    return lax.dot_general(left, right, dims, preferred_element_type=jnp.float32)


def layer_norm(values, gain_row, shift_row):
    center = values - jnp.mean(values, axis=-1, keepdims=True)
    spread = jnp.mean(center * center, axis=-1, keepdims=True)
    return center * lax.rsqrt(spread + epsilon) * gain_row + shift_row


def smooth_gate(values):
    return jax.nn.gelu(values, approximate=True)


def masked_scores(query_block, key_rows, row_first):
    scores = dot(query_block, key_rows, contract_last)
    row_ids = row_first + lax.broadcasted_iota(jnp.int32, scores.shape, 0)
    col_ids = lax.broadcasted_iota(jnp.int32, scores.shape, 1)
    return jnp.where(row_ids >= col_ids, scores, -jnp.inf)


def forward_kernel(query_ref, key_ref, value_ref, blended_ref, logsum_ref):
    length = query_ref.shape[0]
    block_rows = min(BLOCK, length)
    for head in range(2):
        lanes = slice(head * HD, (head + 1) * HD)
        for first in range(0, length, block_rows):
            rows = slice(first, first + block_rows)
            seen = slice(0, first + block_rows)
            query_block = query_ref[rows, lanes] * jnp.bfloat16(HD**-0.5)
            scores = masked_scores(query_block, key_ref[seen, lanes], first)
            largest = jnp.max(scores, axis=-1, keepdims=True)
            weights = jnp.exp(scores - largest)
            totals = jnp.sum(weights, axis=-1, keepdims=True)
            shares = (weights * (1.0 / totals)).astype(jnp.bfloat16)
            blended_ref[rows, lanes] = dot(shares, value_ref[seen, lanes]).astype(jnp.bfloat16)
            logsum_ref[rows, lanes] = jnp.broadcast_to(
                largest + jnp.log(totals), (block_rows, HD)
            )


def backward_kernel(
    query_ref,
    key_ref,
    value_ref,
    change_ref,
    logsum_ref,
    query_change_ref,
    key_change_ref,
    value_change_ref,
    key_sum,
    value_sum,
):
    length = query_ref.shape[0]
    block_rows = min(BLOCK, length)
    key_sum[...] = jnp.zeros_like(key_sum)
    value_sum[...] = jnp.zeros_like(value_sum)
    for head in range(2):
        lanes = slice(head * HD, (head + 1) * HD)
        for first in range(0, length, block_rows):
            rows = slice(first, first + block_rows)
            seen = slice(0, first + block_rows)
            query_block = query_ref[rows, lanes] * jnp.bfloat16(HD**-0.5)
            change_block = change_ref[rows, lanes]
            scores = masked_scores(query_block, key_ref[seen, lanes], first)
            shares = jnp.exp(scores - logsum_ref[rows, lanes][:, :1])
            share_change = dot(change_block, value_ref[seen, lanes], contract_last)
            row_inner = jnp.sum(share_change * shares, axis=-1, keepdims=True)
            score_change = (shares * (share_change - row_inner)).astype(jnp.bfloat16)
            query_change_ref[rows, lanes] = (
                dot(score_change, key_ref[seen, lanes]) * HD**-0.5
            ).astype(jnp.bfloat16)
            key_sum[seen, lanes] += dot(score_change, query_block, contract_rows)
            value_sum[seen, lanes] += dot(
                shares.astype(jnp.bfloat16), change_block, contract_rows
            )
    key_change_ref[...] = key_sum[...].astype(jnp.bfloat16)
    value_change_ref[...] = value_sum[...].astype(jnp.bfloat16)


def pair_spec(length, offset):
    return pl.BlockSpec((length, PAIR), lambda pair: (0, pair + offset))


def attend_forward(projected):
    length, width = projected.shape[0], projected.shape[1] // 3
    pairs = width // PAIR
    return pl.pallas_call(
        forward_kernel,
        grid=(pairs,),
        in_specs=[pair_spec(length, part * pairs) for part in range(3)],
        out_specs=[pair_spec(length, 0)] * 2,
        out_shape=[
            jax.ShapeDtypeStruct((length, width), jnp.bfloat16),
            jax.ShapeDtypeStruct((length, width), jnp.float32),
        ],
        compiler_params=pltpu.CompilerParams(vmem_limit_bytes=32 * 2**20),
        cost_estimate=pl.CostEstimate(
            flops=4 * length * length * width,
            bytes_accessed=12 * length * width,
            transcendentals=length * length * width // HD,
        ),
        name="attend_forward",
    )(projected, projected, projected)


def attend_backward(projected, change, logsum):
    length, width = projected.shape[0], projected.shape[1] // 3
    pairs = width // PAIR
    return pl.pallas_call(
        backward_kernel,
        grid=(pairs,),
        in_specs=[pair_spec(length, part * pairs) for part in range(3)]
        + [pair_spec(length, 0)] * 2,
        out_specs=[pair_spec(length, 0)] * 3,
        out_shape=[jax.ShapeDtypeStruct((length, width), jnp.bfloat16)] * 3,
        scratch_shapes=[pltpu.VMEM((length, PAIR), jnp.float32)] * 2,
        compiler_params=pltpu.CompilerParams(vmem_limit_bytes=32 * 2**20),
        cost_estimate=pl.CostEstimate(
            flops=10 * length * length * width,
            bytes_accessed=18 * length * width,
            transcendentals=length * length * width // HD,
        ),
        name="attend_backward",
    )(projected, projected, projected, change, logsum)


def gathered(block):
    return lax.all_gather(block, "tensor", axis=0, tiled=True)


def scattered(block):
    return lax.psum_scatter(
        block.astype(jnp.bfloat16), "tensor", scatter_dimension=0, tiled=True
    ).astype(jnp.float32)


def swapped(block):
    return lax.ppermute(block, "section", [(0, 1), (1, 0)])


def layer_forward(layer_input, weights):
    attend, mixing, expand, shrink, rows = weights
    gain_one, shift_one, mixing_offset, gain_two, shift_two, shrink_offset = rows[:6]
    attend_offset, expand_offset = rows[6:]
    residual = layer_input.astype(jnp.float32)
    normed = gathered(layer_norm(residual, gain_one, shift_one).astype(jnp.bfloat16))
    projected = (dot(normed, attend) + attend_offset).astype(jnp.bfloat16)
    blended, logsum = attend_forward(projected)
    middle = residual + scattered(dot(blended, mixing)) + mixing_offset
    feed = gathered(layer_norm(middle, gain_two, shift_two).astype(jnp.bfloat16))
    hidden_pre = dot(feed, expand) + expand_offset
    hidden = smooth_gate(hidden_pre).astype(jnp.bfloat16)
    branch = scattered(dot(hidden, shrink, contract_last))
    result = (middle + branch + shrink_offset).astype(jnp.bfloat16)
    return result, (layer_input, normed, projected, logsum, blended, middle, feed, hidden_pre)


def layer_backward(out_change, weights, kept):
    attend, mixing, expand, shrink, rows = weights
    gain_one, shift_one, mixing_offset, gain_two, shift_two, shrink_offset = rows[:6]
    layer_input, normed, projected, logsum, blended, middle, feed, hidden_pre = kept
    gate_value, gate_back = jax.vjp(smooth_gate, hidden_pre)
    hidden = gate_value.astype(jnp.bfloat16)
    change_full = gathered(out_change)
    shrink_change = dot(change_full, hidden, contract_rows).astype(jnp.bfloat16)
    pre_change = gate_back(dot(change_full, shrink))[0].astype(jnp.bfloat16)
    expand_change = dot(feed, pre_change, contract_rows).astype(jnp.bfloat16)
    expand_row_change = jnp.sum(pre_change.astype(jnp.float32), axis=0)
    second_change = scattered(dot(pre_change, expand, contract_last))
    middle_norm, gain_two_change, shift_two_change = jax.vjp(
        layer_norm, middle, gain_two, shift_two
    )[1](second_change)
    out_float = out_change.astype(jnp.float32)
    middle_change = out_float + middle_norm
    branch_full = gathered(middle_change.astype(jnp.bfloat16))
    mixing_change = dot(blended, branch_full, contract_rows).astype(jnp.bfloat16)
    blended_change = dot(branch_full, mixing, contract_last).astype(jnp.bfloat16)
    query_change, key_change, value_change = attend_backward(projected, blended_change, logsum)
    projected_change = jnp.concatenate([query_change, key_change, value_change], axis=1)
    attend_change = dot(normed, projected_change, contract_rows).astype(jnp.bfloat16)
    bias_change = jnp.concatenate(
        [
            jnp.sum(query_change.astype(jnp.float32), axis=0),
            jnp.sum(value_change.astype(jnp.float32), axis=0),
        ]
    )
    first_change = scattered(dot(projected_change, attend, contract_last))
    input_norm, gain_one_change, shift_one_change = jax.vjp(
        layer_norm, layer_input.astype(jnp.float32), gain_one, shift_one
    )[1](first_change)
    input_change = (middle_change + input_norm).astype(jnp.bfloat16)
    row_changes = jnp.stack(
        [
            gain_one_change,
            shift_one_change,
            jnp.sum(middle_change, axis=0),
            gain_two_change,
            shift_two_change,
            jnp.sum(out_float, axis=0),
        ]
    )
    column_changes = jnp.concatenate([bias_change, expand_row_change])
    return (
        input_change,
        (expand_change, shrink_change),
        (attend_change, mixing_change),
        row_changes,
        column_changes,
    )


def total(blocks, after=None):
    if after is not None:
        blocks, after = lax.optimization_barrier((blocks, after))
    sums = lax.psum(blocks, ("section", "dp"))
    return sums, after


def body(
    block_input,
    cotangent,
    first_gain,
    first_shift,
    attend_weight,
    attend_bias,
    mixing_weight,
    mixing_bias,
    second_gain,
    second_shift,
    expand_weight,
    expand_bias,
    shrink_weight,
    shrink_bias,
):
    micro_count, local_rows, model_width = block_input.shape
    local_width = attend_weight.shape[3]
    hidden_width = expand_weight.shape[2]
    section_index = lax.axis_index("section")
    early = section_index == 0

    small = jnp.concatenate(
        [
            first_gain[0],
            first_shift[0],
            mixing_bias[0],
            second_gain[0],
            second_shift[0],
            shrink_bias[0],
            attend_bias[0, 0],
            attend_bias[0, 1],
            expand_bias[0],
        ]
    )
    own = (
        attend_weight[0].reshape(model_width, 3 * local_width),
        mixing_weight[0],
        expand_weight[0],
        shrink_weight[0],
        small,
    )
    other = jax.tree.map(swapped, own)

    def weights_of(layer):
        attend, mixing, expand, shrink, row = (
            jnp.where(early == (layer == 0), mine, theirs) for mine, theirs in zip(own, other)
        )
        row = row.astype(jnp.float32)
        rows = [row[part * model_width : (part + 1) * model_width] for part in range(6)]
        row = row[6 * model_width :]
        blank = jnp.zeros((local_width,), jnp.float32)
        query_offset, value_offset = row[:local_width], row[local_width : 2 * local_width]
        rows.append(jnp.concatenate([query_offset, blank, value_offset]))
        rows.append(row[2 * local_width :])
        return attend, mixing, expand, shrink, rows

    weights = [weights_of(0), weights_of(1)]
    taken = lax.dynamic_index_in_dim(block_input, section_index, 0, keepdims=False)
    given = lax.dynamic_index_in_dim(cotangent, section_index, 0, keepdims=False)

    first_result, first_kept = layer_forward(taken, weights[0])
    second_result, second_kept = layer_forward(first_result, weights[1])
    second_back = layer_backward(given, weights[1], second_kept)
    first_back = layer_backward(second_back[0], weights[0], first_kept)

    def placed(first, second):
        mine = jnp.where(early, first, second)
        theirs = swapped(jnp.where(early, second, first))
        return jnp.stack([jnp.where(early, mine, theirs), jnp.where(early, theirs, mine)])[None]

    section_output = placed(first_result, second_result)
    input_changes = placed(first_back[0], second_back[0])

    late_wide, mark = total(second_back[1])
    late_narrow, mark = total(second_back[2], late_wide)
    soon_wide, mark = total(first_back[1], late_narrow)
    soon_narrow, mark = total(first_back[2], soon_wide)
    columns = lax.psum(jnp.stack([first_back[4], second_back[4]]), ("section", "dp"))
    rows = lax.psum(
        jnp.stack([first_back[3], second_back[3]]), ("section", "dp", "tensor")
    )

    def chosen(first, second):
        return jnp.where(early, first, second).astype(jnp.float32)

    expand_total = chosen(soon_wide[0], late_wide[0])
    shrink_total = chosen(soon_wide[1], late_wide[1])
    attend_total = chosen(soon_narrow[0], late_narrow[0])
    mixing_total = chosen(soon_narrow[1], late_narrow[1])
    column_total = chosen(columns[0], columns[1])
    row_total = chosen(rows[0], rows[1])
    return (
        section_output,
        input_changes,
        row_total[0:1],
        row_total[1:2],
        attend_total.reshape(1, model_width, 3, local_width),
        column_total[: 2 * local_width].reshape(1, 2, local_width),
        mixing_total[None],
        row_total[2:3],
        row_total[3:4],
        row_total[4:5],
        expand_total[None],
        column_total[2 * local_width :][None],
        shrink_total[None],
        row_total[5:6],
    )


def solution(mesh):
    placed = (
        P("dp", "tensor", None),
        P("dp", "tensor", None),
        P("section", None),
        P("section", None),
        P("section", None, None, "tensor"),
        P("section", None, "tensor"),
        P("section", "tensor", None),
        P("section", None),
        P("section", None),
        P("section", None),
        P("section", None, "tensor"),
        P("section", "tensor"),
        P("section", None, "tensor"),
        P("section", None),
    )
    return jax.shard_map(
        body,
        mesh=mesh,
        in_specs=placed,
        out_specs=(
            P("section", "dp", "tensor", None),
            P("section", "dp", "tensor", None),
            P("section", None),
            P("section", None),
            P("section", None, None, "tensor"),
            P("section", None, "tensor"),
            P("section", "tensor", None),
            P("section", None),
            P("section", None),
            P("section", None),
            P("section", None, "tensor"),
            P("section", "tensor"),
            P("section", None, "tensor"),
            P("section", None),
        ),
        check_vma=False,
    )
```

```python
import jax
import jax.numpy as jnp
from jax import lax
from jax.experimental import pallas as pl
from jax.experimental.pallas import tpu as pltpu
from jax.sharding import PartitionSpec as P

HD = 64
PAIR = 2 * HD
BLOCK = 256


epsilon = 1e-05
contract_rows = (((0,), (0,)), ((), ()))
contract_last = (((1,), (1,)), ((), ()))


def dot(left, right, dims=(((1,), (0,)), ((), ()))):
    return lax.dot_general(left, right, dims, preferred_element_type=jnp.float32)


def layer_norm(values, gain_row, shift_row):
    center = values - jnp.mean(values, axis=-1, keepdims=True)
    spread = jnp.mean(center * center, axis=-1, keepdims=True)
    return center * lax.rsqrt(spread + epsilon) * gain_row + shift_row


def smooth_gate(values):
    return jax.nn.gelu(values, approximate=True)


def masked_scores(query_block, key_rows, row_first):
    scores = dot(query_block, key_rows, contract_last)
    row_ids = row_first + lax.broadcasted_iota(jnp.int32, scores.shape, 0)
    col_ids = lax.broadcasted_iota(jnp.int32, scores.shape, 1)
    return jnp.where(row_ids >= col_ids, scores, -jnp.inf)


def forward_kernel(query_ref, key_ref, value_ref, blended_ref, logsum_ref):
    length = query_ref.shape[0]
    block_rows = min(BLOCK, length)
    for head in range(2):
        lanes = slice(head * HD, (head + 1) * HD)
        for first in range(0, length, block_rows):
            rows = slice(first, first + block_rows)
            seen = slice(0, first + block_rows)
            query_block = query_ref[rows, lanes] * jnp.bfloat16(HD**-0.5)
            scores = masked_scores(query_block, key_ref[seen, lanes], first)
            largest = jnp.max(scores, axis=-1, keepdims=True)
            weights = jnp.exp(scores - largest)
            totals = jnp.sum(weights, axis=-1, keepdims=True)
            shares = (weights * (1.0 / totals)).astype(jnp.bfloat16)
            blended_ref[rows, lanes] = dot(shares, value_ref[seen, lanes]).astype(jnp.bfloat16)
            logsum_ref[rows, lanes] = jnp.broadcast_to(
                largest + jnp.log(totals), (block_rows, HD)
            )


def backward_kernel(
    query_ref,
    key_ref,
    value_ref,
    change_ref,
    logsum_ref,
    query_change_ref,
    key_change_ref,
    value_change_ref,
    key_sum,
    value_sum,
):
    length = query_ref.shape[0]
    block_rows = min(BLOCK, length)
    key_sum[...] = jnp.zeros_like(key_sum)
    value_sum[...] = jnp.zeros_like(value_sum)
    for head in range(2):
        lanes = slice(head * HD, (head + 1) * HD)
        for first in range(0, length, block_rows):
            rows = slice(first, first + block_rows)
            seen = slice(0, first + block_rows)
            query_block = query_ref[rows, lanes] * jnp.bfloat16(HD**-0.5)
            change_block = change_ref[rows, lanes]
            scores = masked_scores(query_block, key_ref[seen, lanes], first)
            shares = jnp.exp(scores - logsum_ref[rows, lanes][:, :1])
            share_change = dot(change_block, value_ref[seen, lanes], contract_last)
            row_inner = jnp.sum(share_change * shares, axis=-1, keepdims=True)
            score_change = (shares * (share_change - row_inner)).astype(jnp.bfloat16)
            query_change_ref[rows, lanes] = (
                dot(score_change, key_ref[seen, lanes]) * HD**-0.5
            ).astype(jnp.bfloat16)
            key_sum[seen, lanes] += dot(score_change, query_block, contract_rows)
            value_sum[seen, lanes] += dot(
                shares.astype(jnp.bfloat16), change_block, contract_rows
            )
    key_change_ref[...] = key_sum[...].astype(jnp.bfloat16)
    value_change_ref[...] = value_sum[...].astype(jnp.bfloat16)


def pair_spec(length, offset):
    return pl.BlockSpec((length, PAIR), lambda pair: (0, pair + offset))


def attend_forward(projected):
    length, width = projected.shape[0], projected.shape[1] // 3
    pairs = width // PAIR
    return pl.pallas_call(
        forward_kernel,
        grid=(pairs,),
        in_specs=[pair_spec(length, part * pairs) for part in range(3)],
        out_specs=[pair_spec(length, 0)] * 2,
        out_shape=[
            jax.ShapeDtypeStruct((length, width), jnp.bfloat16),
            jax.ShapeDtypeStruct((length, width), jnp.float32),
        ],
        compiler_params=pltpu.CompilerParams(vmem_limit_bytes=32 * 2**20),
        cost_estimate=pl.CostEstimate(
            flops=4 * length * length * width,
            bytes_accessed=12 * length * width,
            transcendentals=length * length * width // HD,
        ),
        name="attend_forward",
    )(projected, projected, projected)


def attend_backward(projected, change, logsum):
    length, width = projected.shape[0], projected.shape[1] // 3
    pairs = width // PAIR
    return pl.pallas_call(
        backward_kernel,
        grid=(pairs,),
        in_specs=[pair_spec(length, part * pairs) for part in range(3)]
        + [pair_spec(length, 0)] * 2,
        out_specs=[pair_spec(length, 0)] * 3,
        out_shape=[jax.ShapeDtypeStruct((length, width), jnp.bfloat16)] * 3,
        scratch_shapes=[pltpu.VMEM((length, PAIR), jnp.float32)] * 2,
        compiler_params=pltpu.CompilerParams(vmem_limit_bytes=32 * 2**20),
        cost_estimate=pl.CostEstimate(
            flops=10 * length * length * width,
            bytes_accessed=18 * length * width,
            transcendentals=length * length * width // HD,
        ),
        name="attend_backward",
    )(projected, projected, projected, change, logsum)


def gathered(block):
    return lax.all_gather(block, "tensor", axis=0, tiled=True)


def scattered(block):
    return lax.psum_scatter(
        block.astype(jnp.bfloat16), "tensor", scatter_dimension=0, tiled=True
    ).astype(jnp.float32)


def gathered_early(block):
    size, place = lax.axis_size("tensor"), lax.axis_index("tensor")
    rows = block.shape[0]
    whole = jnp.zeros((size * rows, block.shape[1]), block.dtype)
    for step in range(size):
        route = [(i, (i + step) % size) for i in range(size)]
        piece = lax.ppermute(block, "tensor", route) if step else block
        origin = lax.rem(place - step + size, size)
        whole = lax.dynamic_update_slice_in_dim(whole, piece, origin * rows, 0)
    return whole


def partner(block, distance):
    return lax.ppermute(block, "dp", [(i, i ^ distance) for i in range(lax.axis_size("dp"))])


def joined(block, other, bit):
    lower = jnp.where(bit == 0, block, other)
    upper = jnp.where(bit == 0, other, block)
    return jnp.concatenate([lower, upper], axis=0)


def half_of(block, which):
    rows = block.shape[0] // 2
    return lax.dynamic_slice_in_dim(block, which * rows, rows, 0)


def swapped(block):
    return lax.ppermute(block, "section", [(0, 1), (1, 0)])


def fetched(block):
    core = lax.rem(lax.axis_index("dp"), 2)
    got = swapped(half_of(block, core))
    return joined(got, partner(got, 1), core)


def total(block, owner):
    place = lax.axis_index("dp")
    distances = []
    while 2 ** len(distances) < lax.axis_size("dp"):
        distances.append(2 ** len(distances))
    for distance in distances:
        bit = lax.rem(place // distance, 2)
        got = partner(half_of(block, 1 - bit), distance)
        block = (half_of(block, bit).astype(jnp.float32) + got.astype(jnp.float32)).astype(
            block.dtype
        )
    got = lax.ppermute(block, "section", [(1 - owner, owner)])
    block = (block.astype(jnp.float32) + got.astype(jnp.float32)).astype(block.dtype)
    for distance in reversed(distances):
        bit = lax.rem(place // distance, 2)
        block = joined(block, partner(block, distance), bit)
    return block


def layer_forward(layer_input, weights):
    attend, mixing, expand, shrink, rows = weights
    gain_one, shift_one, mixing_offset, gain_two, shift_two, shrink_offset = rows[:6]
    attend_offset, expand_offset = rows[6:]
    residual = layer_input.astype(jnp.float32)
    normed = gathered(layer_norm(residual, gain_one, shift_one).astype(jnp.bfloat16))
    projected = (dot(normed, attend) + attend_offset).astype(jnp.bfloat16)
    blended, logsum = attend_forward(projected)
    mixed = scattered(dot(blended, mixing))
    mixed, expand, shrink = lax.optimization_barrier((mixed, expand, shrink))
    middle = residual + mixed + mixing_offset
    feed = gathered(layer_norm(middle, gain_two, shift_two).astype(jnp.bfloat16))
    hidden_pre = dot(feed, expand) + expand_offset
    hidden = smooth_gate(hidden_pre).astype(jnp.bfloat16)
    branch = scattered(dot(hidden, shrink, contract_last))
    result = (middle + branch + shrink_offset).astype(jnp.bfloat16)
    return result, (layer_input, normed, projected, logsum, blended, middle, feed, hidden_pre)


def layer_backward(out_change, change_full, weights, kept):
    attend, mixing, expand, shrink, rows = weights
    gain_one, shift_one, mixing_offset, gain_two, shift_two, shrink_offset = rows[:6]
    layer_input, normed, projected, logsum, blended, middle, feed, hidden_pre = kept
    gate_value, gate_back = jax.vjp(smooth_gate, hidden_pre)
    hidden = gate_value.astype(jnp.bfloat16)
    shrink_change = dot(change_full, hidden, contract_rows).astype(jnp.bfloat16)
    pre_change = gate_back(dot(change_full, shrink))[0].astype(jnp.bfloat16)
    expand_change = dot(feed, pre_change, contract_rows).astype(jnp.bfloat16)
    expand_row_change = jnp.sum(pre_change.astype(jnp.float32), axis=0)
    second_change = scattered(dot(pre_change, expand, contract_last))
    middle_norm, gain_two_change, shift_two_change = jax.vjp(
        layer_norm, middle, gain_two, shift_two
    )[1](second_change)
    out_float = out_change.astype(jnp.float32)
    middle_change = out_float + middle_norm
    branch_full = gathered(middle_change.astype(jnp.bfloat16))
    mixing_change = dot(blended, branch_full, contract_rows).astype(jnp.bfloat16)
    blended_change = dot(branch_full, mixing, contract_last).astype(jnp.bfloat16)
    query_change, key_change, value_change = attend_backward(projected, blended_change, logsum)
    projected_change = jnp.concatenate([query_change, key_change, value_change], axis=1)
    attend_change = dot(normed, projected_change, contract_rows).astype(jnp.bfloat16)
    bias_change = jnp.concatenate(
        [
            jnp.sum(query_change.astype(jnp.float32), axis=0),
            jnp.sum(value_change.astype(jnp.float32), axis=0),
        ]
    )
    first_change = scattered(dot(projected_change, attend, contract_last))
    input_norm, gain_one_change, shift_one_change = jax.vjp(
        layer_norm, layer_input.astype(jnp.float32), gain_one, shift_one
    )[1](first_change)
    input_change = (middle_change + input_norm).astype(jnp.bfloat16)
    row_changes = jnp.stack(
        [
            gain_one_change,
            shift_one_change,
            jnp.sum(middle_change, axis=0),
            gain_two_change,
            shift_two_change,
            jnp.sum(out_float, axis=0),
        ]
    )
    column_changes = jnp.concatenate([bias_change, expand_row_change])
    return (
        input_change,
        jnp.concatenate([expand_change, shrink_change], axis=0),
        jnp.concatenate([attend_change.reshape(-1, mixing.shape[1]), mixing_change], axis=0),
        row_changes,
        column_changes,
    )


def body(
    block_input,
    cotangent,
    first_gain,
    first_shift,
    attend_weight,
    attend_bias,
    mixing_weight,
    mixing_bias,
    second_gain,
    second_shift,
    expand_weight,
    expand_bias,
    shrink_weight,
    shrink_bias,
):
    micro_count, local_rows, model_width = block_input.shape
    local_width = attend_weight.shape[3]
    section_index = lax.axis_index("section")
    early = section_index == 0

    small = jnp.concatenate(
        [
            first_gain[0],
            first_shift[0],
            mixing_bias[0],
            second_gain[0],
            second_shift[0],
            shrink_bias[0],
            attend_bias[0, 0],
            attend_bias[0, 1],
            expand_bias[0],
        ]
    )
    own = (
        attend_weight[0].reshape(model_width, 3 * local_width),
        mixing_weight[0],
        expand_weight[0],
        shrink_weight[0],
        small,
    )
    other = tuple(fetched(block) for block in own[:4]) + (swapped(small),)

    def weights_of(layer):
        attend, mixing, expand, shrink, row = (
            jnp.where(early == (layer == 0), mine, theirs) for mine, theirs in zip(own, other)
        )
        row = row.astype(jnp.float32)
        rows = [row[part * model_width : (part + 1) * model_width] for part in range(6)]
        row = row[6 * model_width :]
        blank = jnp.zeros((local_width,), jnp.float32)
        query_offset, value_offset = row[:local_width], row[local_width : 2 * local_width]
        rows.append(jnp.concatenate([query_offset, blank, value_offset]))
        rows.append(row[2 * local_width :])
        return attend, mixing, expand, shrink, rows

    weights = [weights_of(0), weights_of(1)]
    taken = lax.dynamic_index_in_dim(block_input, section_index, 0, keepdims=False)
    given = lax.dynamic_index_in_dim(cotangent, section_index, 0, keepdims=False)

    first_result, first_kept = layer_forward(taken, weights[0])
    second_result, second_kept = layer_forward(first_result, weights[1])
    second_back = layer_backward(given, gathered_early(given), weights[1], second_kept)
    first_back = layer_backward(
        second_back[0], gathered(second_back[0]), weights[0], first_kept
    )

    def placed(first, second):
        earlier = lax.ppermute(first, "section", [(1, 0)])
        later = lax.ppermute(second, "section", [(0, 1)])
        return jnp.where(early, jnp.stack([first, earlier]), jnp.stack([later, second]))[None]

    section_output = placed(first_result, second_result)
    input_changes = placed(first_back[0], second_back[0])

    wide = [total(first_back[1], 0), total(second_back[1], 1)]
    narrow = [total(first_back[2], 0), total(second_back[2], 1)]

    shards, shard = lax.axis_size("tensor"), lax.axis_index("tensor")
    row_changes = jnp.stack([first_back[3], second_back[3]])
    column_changes = jnp.stack([first_back[4], second_back[4]])
    spread = jnp.where(
        (jnp.arange(shards) == shard)[:, None], column_changes.reshape(1, -1), 0.0
    )
    sums = lax.psum(
        jnp.concatenate([row_changes.reshape(-1), spread.reshape(-1)]),
        ("section", "dp", "tensor"),
    )
    rows = sums[: row_changes.size].reshape(row_changes.shape)
    columns = lax.dynamic_index_in_dim(
        sums[row_changes.size :].reshape(spread.shape), shard, 0, keepdims=False
    ).reshape(column_changes.shape)

    def chosen(first, second):
        return jnp.where(early, first, second).astype(jnp.float32)

    wide_total = chosen(*wide)
    narrow_total = chosen(*narrow)
    expand_total, shrink_total = wide_total[:model_width], wide_total[model_width:]
    attend_rows = 3 * local_width
    attend_total, mixing_total = narrow_total[:attend_rows], narrow_total[attend_rows:]
    column_total = chosen(columns[0], columns[1])
    row_total = chosen(rows[0], rows[1])
    return (
        section_output,
        input_changes,
        row_total[0:1],
        row_total[1:2],
        attend_total.reshape(1, model_width, 3, local_width),
        column_total[: 2 * local_width].reshape(1, 2, local_width),
        mixing_total[None],
        row_total[2:3],
        row_total[3:4],
        row_total[4:5],
        expand_total[None],
        column_total[2 * local_width :][None],
        shrink_total[None],
        row_total[5:6],
    )


def solution(mesh):
    placed = (
        P("dp", "tensor", None),
        P("dp", "tensor", None),
        P("section", None),
        P("section", None),
        P("section", None, None, "tensor"),
        P("section", None, "tensor"),
        P("section", "tensor", None),
        P("section", None),
        P("section", None),
        P("section", None),
        P("section", None, "tensor"),
        P("section", "tensor"),
        P("section", None, "tensor"),
        P("section", None),
    )
    return jax.shard_map(
        body,
        mesh=mesh,
        in_specs=placed,
        out_specs=(
            P("section", "dp", "tensor", None),
            P("section", "dp", "tensor", None),
            P("section", None),
            P("section", None),
            P("section", None, None, "tensor"),
            P("section", None, "tensor"),
            P("section", "tensor", None),
            P("section", None),
            P("section", None),
            P("section", None),
            P("section", None, "tensor"),
            P("section", "tensor"),
            P("section", None, "tensor"),
            P("section", None),
        ),
        check_vma=False,
    )
```
